256 devices in a mesh: dp: 16 (over z_lo, y), hidden: 16 (over x, z_hi, core).
Axes of the slice: x: 4, y: 4, z: 8 (z_hi: 2, z_lo: 4; z = z_hi * 4 + z_lo), core: 2. Of those that a mesh axis runs over, the one named last changes fastest.
Arguments:
- activations: bfloat16 [4, 128, 8192], P(None, 'hidden', 'dp'), may hold values from -6 to 6
- out_grad: bfloat16 [4, 128, 8192], P(None, 'hidden', 'dp'), may hold values from -6 to 6
- w_gate: bfloat16 [8192, 28672], P('dp', 'hidden'), may hold values from -0.0625 to 0.0625
- w_up: bfloat16 [8192, 28672], P('dp', 'hidden'), may hold values from -0.0625 to 0.0625
- w_down: bfloat16 [28672, 8192], P('hidden', 'dp'), may hold values from -0.03125 to 0.03125
- levels: int32 [4], replicated, may hold values from 0 to 3, each once
Outputs:
- input_grad: bfloat16 [4, 128, 8192], P(None, 'hidden', 'dp')
- gate_grad: bfloat16 [8192, 28672], P('dp', 'hidden')
- up_grad: bfloat16 [8192, 28672], P('dp', 'hidden')
- down_grad: bfloat16 [28672, 8192], P('hidden', 'dp')
The draws below stay inside these ranges and needn't reach their ends.
Inputs may be any that keep to these rules, and one draw needn't show every extreme that they name: Each of 0 to 3 appears once; micro-batch b uses the first (3584) * 2 ** levels[b] hidden units.
All inputs are finite; a program needn't handle non-finite values.
Results may differ from the reference program's by a relative error of at most 0.005.
Values may be sent and summed in bfloat16 or wider, within the bound.
A program may use at most 128 MiB of HBM per device.

```python
import jax
import jax.numpy as jnp

D = 8192
FF = 28672
LEVELS = 4
MICRO = 128
ROWS = 512


def steps_of(key, shape, split, least, largest):
    level, own = 1.0, jax.random.fold_in(key, 6)
    for dim, parts in split:
        steps = jnp.exp(jax.random.uniform(jax.random.fold_in(own, dim), (parts,), jnp.float32, least / len(split), largest / len(split)))
        level = level * jnp.repeat(steps, shape[dim] // parts).reshape([-1 if axis == dim else 1 for axis in range(len(shape))])
    return level


def gaussian(key, dims, width, limit, shards=(), kind=jnp.bfloat16):
    drawn = jax.random.normal(key, dims, jnp.float32) * width
    if len(shards) > 0:
        drawn = steps_of(key, dims, shards, -0.22, 0.18) * drawn
    return jnp.clip(drawn, min=-limit, max=limit).astype(kind)


def setup_inputs(seed: int = 0) -> dict:
    key_list = jax.random.split(jax.random.key(seed), 7)
    return {
        "activations": gaussian(key_list[0], (LEVELS, MICRO, D), 1.0, 6.0, ((1, 16), (2, 16))),
        "out_grad": gaussian(key_list[1], (LEVELS, MICRO, D), 1.0, 6.0, ((1, 16), (2, 16))),
        "w_gate": gaussian(key_list[2], (D, FF), D ** -0.5, 0.0625, ((0, 16), (1, 16))),
        "w_up": gaussian(key_list[3], (D, FF), D ** -0.5, 0.0625, ((0, 16), (1, 16))),
        "w_down": gaussian(key_list[4], (FF, D), FF ** -0.5, 0.03125, ((0, 16), (1, 16))),
        "levels": jax.random.permutation(key_list[5], LEVELS).astype(jnp.int32),
    }


def reference(activations, out_grad, w_gate, w_up, w_down, levels):
    rows = activations.reshape(ROWS, D)
    grad_rows = out_grad.reshape(ROWS, D)
    level_row = jnp.repeat(levels, MICRO)
    limit_row = jnp.left_shift(jnp.ones_like(level_row), level_row) * (FF // 8)
    columns = jnp.arange(FF, dtype=jnp.int32)
    active = columns[None, :] < limit_row[:, None]
    gate_sum = jnp.dot(rows, w_gate, preferred_element_type=jnp.float32)
    up_sum = jnp.dot(rows, w_up, preferred_element_type=jnp.float32)
    hidden_grad = jnp.dot(grad_rows, w_down.T, preferred_element_type=jnp.float32)
    sigmoid_gate = jax.nn.sigmoid(gate_sum)
    zero_value = jnp.zeros_like(gate_sum)
    hidden_act = jnp.where(active, gate_sum * sigmoid_gate * up_sum, zero_value).astype(jnp.bfloat16)
    masked_grad = jnp.where(active, hidden_grad, zero_value)
    dgate = (masked_grad * up_sum * sigmoid_gate * (1.0 + gate_sum * (1.0 - sigmoid_gate))).astype(jnp.bfloat16)
    dup = (masked_grad * gate_sum * sigmoid_gate).astype(jnp.bfloat16)
    gate_grad = jnp.dot(rows.T, dgate, preferred_element_type=jnp.float32).astype(jnp.bfloat16)
    up_grad = jnp.dot(rows.T, dup, preferred_element_type=jnp.float32).astype(jnp.bfloat16)
    down_grad = jnp.dot(hidden_act.T, grad_rows, preferred_element_type=jnp.float32).astype(jnp.bfloat16)
    input_sum = jnp.dot(dgate, w_gate.T, preferred_element_type=jnp.float32) + jnp.dot(dup, w_up.T, preferred_element_type=jnp.float32)
    input_grad = input_sum.astype(jnp.bfloat16).reshape(LEVELS, MICRO, D)
    return input_grad, gate_grad, up_grad, down_grad
```

```python
import functools

import jax
import jax.numpy as jnp
from jax import lax
from jax.experimental import pallas as pl
from jax.experimental.pallas import tpu as pltpu
from jax.sharding import PartitionSpec as P

MESH = pl.DeviceIdType.MESH
BF16 = jnp.bfloat16
F32 = jnp.float32

UNITS = 4
TOK = 128
FEAT = 512
WIDTH = 1792
HALF = WIDTH // 2
TILE = 256
CHIPS = 8
NT = (((1,), (1,)), ((), ()))


def device(z, y, chip, core):
    return (z * 4 + y, chip * 2 + core)


def active_count(chip):
    return 1 + (chip < 4).astype(jnp.int32) + (chip < 2) + (chip < 1)


def kernel(
    lev, x_ref, g_ref, wg_hbm, wu_hbm, wd_hbm,
    in_grad, x_out, g_out, act_hbm, dg_hbm, du_hbm,
    wg, wu, wd, own, pair, xg, pf, pb, r1, r2, zr, agb, term, pair_t, hr, fs, fr,
    w_sem, o_sem, a_send, a_recv, s_send, s_recv, h_send, h_recv,
):
    dp = lax.axis_index("dp")
    hidden = lax.axis_index("hidden")
    z, y = dp // 4, dp % 4
    chip, core = hidden // 2, hidden % 2
    xx, zh = chip // 2, chip % 2
    other = 1 - core
    n = active_count(chip)
    y_opp, y_right, y_left = (y + 2) % 4, (y + 1) % 4, (y + 3) % 4
    partner = device(z, y, chip, other)
    right, left = device(z, y_right, chip, core), device(z, y_left, chip, core)

    def remote(src, dst, send, recv, target):
        return pltpu.make_async_remote_copy(
            src_ref=src, dst_ref=dst, send_sem=send, recv_sem=recv, device_id=target, device_id_type=MESH
        )

    loads = [
        pltpu.make_async_copy(src, dst, w_sem.at[k])
        for k, (src, dst) in enumerate(((wg_hbm, wg), (wu_hbm, wu), (wd_hbm, wd)))
    ]
    for load in loads:
        load.start()

    barrier = pltpu.get_barrier_semaphore()
    greeted = [partner, right, left]
    greeted += [device((z + k) % 4, y, chip, core) for k in (1, 2, 3)]
    greeted += [device(z, y, (chip + k) % CHIPS, core) for k in range(1, CHIPS)]
    for who in greeted:
        pl.semaphore_signal(barrier, inc=1, device_id=who, device_id_type=MESH)

    for array, ref in enumerate((x_ref, g_ref)):
        rows = []
        for u in range(UNITS):
            index = jnp.int32(0)
            for i in range(1, UNITS):
                index = jnp.where(lev[i] == UNITS - 1 - u, i, index)
            rows.append(ref[index].astype(F32))
        own[array * 32 : array * 32 + 16] = jnp.concatenate(rows[:2], 0).astype(BF16)
        own[array * 32 + 16 : array * 32 + 32] = jnp.concatenate(rows[2:], 0).astype(BF16)

    pl.semaphore_wait(barrier, len(greeted))

    pair_copy = remote(own, pair, a_send.at[0], a_recv.at[0], partner)
    pair_copy.start()
    pair_copy.wait()
    for u in range(0, UNITS, 2):
        rows = pl.ds(pl.multiple_of(core * 32 + u * 8, 16), 16)
        mine, theirs = own[rows].astype(F32), pair[rows].astype(F32)
        zero = jnp.where(core == 0, mine, theirs)
        one = jnp.where(core == 0, theirs, mine)
        xg[core, u, chip] = jnp.concatenate([zero[:8], one[:8]], 0).astype(BF16)
        xg[core, u + 1, chip] = jnp.concatenate([zero[8:], one[8:]], 0).astype(BF16)

    def block(c):
        return xg.at[core, :, c]

    far = 2 * xx + (1 - zh)
    spread = [remote(block(chip), block(chip), a_send.at[1], a_recv.at[1], device(z, y, far, core))]
    for k in (1, 2, 3):
        target = device(z, y, 2 * ((xx + k) % 4) + zh, core)
        spread.append(remote(block(chip), block(chip), a_send.at[1 + k], a_recv.at[1 + k], target))
    for copy in spread:
        copy.start()
    spread[0].wait_recv()
    for k in (1, 2, 3):
        target = device(z, y, 2 * ((xx + k) % 4) + zh, core)
        spread.append(remote(block(far), block(far), a_send.at[4 + k], a_recv.at[4 + k], target))
        spread[-1].start()
    for copy in spread[1:]:
        copy.wait_recv()
    for copy in spread:
        copy.wait_send()
    swap = remote(xg.at[core], xg.at[core], a_send.at[8], a_recv.at[8], partner)
    swap.start()
    swap.wait()
    for load in loads:
        load.wait()

    def own_piece(ref, u):
        return ref.at[u, :, pl.ds(y * 32 + (z // 2) * 16, 16), pl.ds(pl.multiple_of((z % 2) * HALF, HALF), HALF)]

    def part(ref, u, yy, half, count=16):
        return ref.at[u, :, pl.ds(yy * 32 + half * 16, count), :]

    def copy_of(u, kind):
        if kind == 0:
            src, dst, to = part(pb, u, y_opp, 0), r1.at[u, 0], right
        elif kind == 1:
            src, dst, to = part(pb, u, y_opp, 1), r1.at[u, 1], left
        elif kind == 2:
            src, dst, to = part(pb, u, y_right, 1), r2.at[u, 0, :, pl.ds(16, 16), :], right
        elif kind == 3:
            src, dst, to = part(pb, u, y_left, 0), r2.at[u, 1, :, pl.ds(0, 16), :], left
        elif kind == 4:
            src, dst, to = r1.at[u, 0], r2.at[u, 0, :, pl.ds(0, 16), :], right
        elif kind == 5:
            src, dst, to = r1.at[u, 1], r2.at[u, 1, :, pl.ds(16, 16), :], left
        elif kind in (6, 7, 8):
            zd = (z + kind - 5) % 4
            src = pf.at[
                u, :, pl.ds(y * 32 + (zd // 2) * 16, 16), pl.ds(pl.multiple_of((zd % 2) * HALF, HALF), HALF)
            ]
            dst, to = zr.at[u, kind - 6], device(zd, y, chip, core)
        elif kind in (9, 10, 11):
            src = dst = own_piece(agb, u)
            to = device((z + kind - 8) % 4, y, chip, core)
        elif kind == 12:
            src, to = part(agb, u, y, 0, 32), right
            dst = src
        elif kind == 13:
            src, to = part(agb, u, y, 0, 32), left
            dst = src
        elif kind == 14:
            src, to = part(agb, u, y_left, 0), right
            dst = src
        else:
            src, to = part(agb, u, y_right, 1), left
            dst = src
        return remote(src, dst, s_send.at[u, kind], s_recv.at[u, kind], to)

    def pair_term(u):
        return remote(term.at[u, other], pair_t.at[u], h_send.at[u, 7], h_recv.at[u, 8], partner)

    def chip_term(u, k):
        target = (chip + k) % CHIPS
        return remote(
            term.at[u, core, pl.ds(target * 16, 16), :], hr.at[u, chip],
            h_send.at[u, k - 1], h_recv.at[u, chip], device(z, y, target, core),
        )

    def dots(u):
        def tile(i, _):
            cols = pl.ds(pl.multiple_of(i * TILE, TILE), TILE)
            rows_x = xg[0, u].reshape(TOK, FEAT)
            rows_g = xg[1, u].reshape(TOK, FEAT)
            values = (
                jnp.dot(rows_x, wg[:, cols], preferred_element_type=F32),
                jnp.dot(rows_x, wu[:, cols], preferred_element_type=F32),
                lax.dot_general(rows_g, wd[cols, :], NT, preferred_element_type=F32),
            )
            for k, value in enumerate(values):
                pf[u, k, :, cols] = value
                pb[u, k, :, cols] = value.astype(BF16)
            return 0

        lax.fori_loop(0, WIDTH // TILE, tile, 0)
        for kind in range(4):
            copy_of(u, kind).start()

    def accumulate(u):
        for side, (kind, yy) in enumerate(((0, y_right), (1, y_left))):
            copy_of(u, kind).wait_recv()
            rows = pl.ds(yy * 32 + side * 16, 16)
            for k in range(3):
                r1[u, side, k] = (r1[u, side, k].astype(F32) + pf[u, k, rows, :]).astype(BF16)
            copy_of(u, kind + 4).start()

    def sum_y(u):
        for kind in (2, 3, 4, 5):
            copy_of(u, kind).wait_recv()
        rows = pl.ds(y * 32, 32)
        for k in range(3):
            pf[u, k, rows, :] += r2[u, 0, k].astype(F32) + r2[u, 1, k].astype(F32)
        for kind in (6, 7, 8):
            copy_of(u, kind).start()

    def units(u):
        for kind in (6, 7, 8):
            copy_of(u, kind).wait_recv()
        rows = pl.ds(y * 32 + (z // 2) * 16, 16)
        cols = pl.ds(pl.multiple_of((z % 2) * HALF, HALF), HALF)
        gate, up, grad = (
            pf[u, k, rows, cols] + (zr[u, 0, k] + zr[u, 1, k] + zr[u, 2, k]) for k in range(3)
        )
        s = jax.nn.sigmoid(gate)
        agb[u, 0, rows, cols] = (gate * s * up).astype(BF16)
        agb[u, 1, rows, cols] = (grad * up * s * (1.0 + gate * (1.0 - s))).astype(BF16)
        agb[u, 2, rows, cols] = (grad * gate * s).astype(BF16)
        for kind in (9, 10, 11):
            copy_of(u, kind).start()

    def spread_y(u):
        for kind in (9, 10, 11):
            copy_of(u, kind).wait_recv()
        for kind in (12, 13):
            copy_of(u, kind).start()

    def forward_y(u):
        for kind in (12, 13):
            copy_of(u, kind).wait_recv()
            copy_of(u, kind + 2).start()

    def save(u, k):
        out = (act_hbm, dg_hbm, du_hbm)[k]
        return pltpu.make_async_copy(agb.at[u, k], out.at[pl.ds(u * TOK, TOK), :], o_sem.at[u, k])

    def back(u):
        for kind in (14, 15):
            copy_of(u, kind).wait_recv()
        for half in range(2):
            feats = slice(half * TILE, half * TILE + TILE)
            term[u, half] = lax.dot_general(
                agb[u, 1], wg[feats, :], NT, preferred_element_type=F32
            ) + lax.dot_general(agb[u, 2], wu[feats, :], NT, preferred_element_type=F32)
        pair_term(u).start()
        for k in range(3):
            save(u, k).start()

    def send_terms(u):
        pair_term(u).wait_recv()
        term[u, core] += pair_t[u]
        for k in range(1, CHIPS):
            chip_term(u, k).start()

    stages = (dots, accumulate, sum_y, units, spread_y, forward_y, back, send_terms)

    def step(t, _):
        for lag in reversed(range(len(stages))):
            u = t - lag

            @pl.when(jnp.logical_and(u >= 0, u < n))
            def _(u=u, lag=lag):
                stages[lag](u)

        return 0

    lax.fori_loop(0, n + len(stages) - 1, step, 0)

    def clear(u, _):
        agb[u] = jnp.zeros((3, TOK, WIDTH), BF16)
        for k in range(3):
            save(u, k).start()
        return 0

    lax.fori_loop(n, UNITS, clear, 0)

    for u in range(UNITS):
        fs[u] = jnp.zeros((16, TILE), F32)

        def add(j, _, u=u):
            @pl.when(j == chip)
            def _():
                fs[u] += term[u, core, pl.ds(chip * 16, 16), :]

            @pl.when(j != chip)
            def _():
                remote(
                    hr.at[u, j], hr.at[u, j], h_send.at[u, 0], h_recv.at[u, j], device(z, y, j, core)
                ).wait_recv()
                fs[u] += hr[u, j]

            return 0

        lax.fori_loop(0, (8, 4, 2, 1)[u], add, 0)

    last = remote(
        fs.at[:, pl.ds(pl.multiple_of(other * 8, 8), 8), :], fr, a_send.at[9], a_recv.at[9], partner
    )
    last.start()
    last.wait()
    here = pl.ds(pl.multiple_of(core * TILE, TILE), TILE)
    there = pl.ds(pl.multiple_of(other * TILE, TILE), TILE)
    mine = pl.ds(pl.multiple_of(core * 8, 8), 8)
    for b in range(UNITS):
        u = UNITS - 1 - lev[b]
        in_grad[b, :, here] = fs[u, mine, :].astype(BF16)
        in_grad[b, :, there] = fr[u].astype(BF16)
    x_out[...] = xg[0].reshape(UNITS * TOK, FEAT)
    g_out[...] = xg[1].reshape(UNITS * TOK, FEAT)

    def drain(u, _):
        for kind in range(16):
            copy_of(u, kind).wait_send()
        pair_term(u).wait_send()
        for k in range(1, CHIPS):
            chip_term(u, k).wait_send()
        return 0

    lax.fori_loop(0, n, drain, 0)
    for u in range(UNITS):
        for k in range(3):
            save(u, k).wait()


def exchange(levels, activations, out_grad, w_gate, w_up, w_down):
    rows = UNITS * TOK
    vmem = pl.BlockSpec(memory_space=pltpu.VMEM)
    hbm = pl.BlockSpec(memory_space=pl.ANY)
    dma = pltpu.SemaphoreType.DMA
    return pl.pallas_call(
        kernel,
        out_shape=[
            jax.ShapeDtypeStruct(activations.shape, BF16),
            jax.ShapeDtypeStruct((rows, FEAT), BF16),
            jax.ShapeDtypeStruct((rows, FEAT), BF16),
            jax.ShapeDtypeStruct((rows, WIDTH), BF16),
            jax.ShapeDtypeStruct((rows, WIDTH), BF16),
            jax.ShapeDtypeStruct((rows, WIDTH), BF16),
        ],
        in_specs=[pl.BlockSpec(memory_space=pltpu.SMEM), vmem, vmem, hbm, hbm, hbm],
        out_specs=[vmem, vmem, vmem, hbm, hbm, hbm],
        scratch_shapes=[
            pltpu.VMEM((FEAT, WIDTH), BF16),
            pltpu.VMEM((FEAT, WIDTH), BF16),
            pltpu.VMEM((WIDTH, FEAT), BF16),
            pltpu.VMEM((64, FEAT), BF16),
            pltpu.VMEM((64, FEAT), BF16),
            pltpu.VMEM((2, UNITS, CHIPS, 16, FEAT), BF16),
            pltpu.VMEM((UNITS, 3, TOK, WIDTH), F32),
            pltpu.VMEM((UNITS, 3, TOK, WIDTH), BF16),
            pltpu.VMEM((UNITS, 2, 3, 16, WIDTH), BF16),
            pltpu.VMEM((UNITS, 2, 3, 32, WIDTH), BF16),
            pltpu.VMEM((UNITS, 3, 3, 16, HALF), F32),
            pltpu.VMEM((UNITS, 3, TOK, WIDTH), BF16),
            pltpu.VMEM((UNITS, 2, TOK, TILE), F32),
            pltpu.VMEM((UNITS, TOK, TILE), F32),
            pltpu.VMEM((UNITS, CHIPS, 16, TILE), F32),
            pltpu.VMEM((UNITS, 16, TILE), F32),
            pltpu.VMEM((UNITS, 8, TILE), F32),
            dma((3,)),
            dma((UNITS, 3)),
            dma((10,)),
            dma((10,)),
            dma((UNITS, 16)),
            dma((UNITS, 16)),
            dma((UNITS, 8)),
            dma((UNITS, 9)),
        ],
        compiler_params=pltpu.CompilerParams(
            collective_id=0, has_side_effects=True, vmem_limit_bytes=56 * 1024 * 1024
        ),
    )(levels, activations, out_grad, w_gate, w_up, w_down)


def body(activations, out_grad, w_gate, w_up, w_down, levels):
    input_grad, rows_x, rows_g, act, dgate, dup = exchange(
        levels, activations, out_grad, w_gate, w_up, w_down
    )
    contract_rows = (((0,), (0,)), ((), ()))
    dot = functools.partial(
        lax.dot_general, dimension_numbers=contract_rows, preferred_element_type=F32
    )
    return (
        input_grad,
        dot(rows_x, dgate).astype(BF16),
        dot(rows_x, dup).astype(BF16),
        dot(act, rows_g).astype(BF16),
    )


def solution(mesh):
    placed = (
        P(None, "hidden", "dp"),
        P(None, "hidden", "dp"),
        P("dp", "hidden"),
        P("dp", "hidden"),
        P("hidden", "dp"),
        P(),
    )
    return jax.shard_map(
        body,
        mesh=mesh,
        in_specs=placed,
        out_specs=(
            P(None, "hidden", "dp"),
            P("dp", "hidden"),
            P("dp", "hidden"),
            P("hidden", "dp"),
        ),
        check_vma=False,
    )
```

```python
import jax
import jax.numpy as jnp
from jax import lax
from jax.experimental import pallas as pl
from jax.experimental.pallas import tpu as pltpu
from jax.sharding import PartitionSpec as P

MESH = pl.DeviceIdType.MESH
BF16 = jnp.bfloat16
F32 = jnp.float32

UNITS = 4
TOK = 128
FEAT = 512
WIDTH = 1792
TILE = 256
CHIPS = 8
SPANS = ((0, 512), (512, 512), (1024, 768))
LENT = {(3, 0): 1, (3, 1): 3, (3, 2): 2}
NT = (((1,), (1,)), ((), ()))
ORDER_LENDER = (3, 2, 1, 0)
ORDER = (0, 3, 1, 2)
LAGS = (0, 2, 4, 6, 8, 10, 12, 14)


def device(z, y, chip, core):
    return (z * 4 + y, chip * 2 + core)


def active_count(chip):
    return 1 + (chip < 4).astype(jnp.int32) + (chip < 2) + (chip < 1)


def kernel(
    lev, x_ref, g_ref, wg_hbm, wu_hbm, wd_hbm,
    in_grad, gate_hbm, up_hbm, down_hbm,
    wg, wu, wd, own, pair, xg, pf, pb, r1, r2, zr, zs, zx, agb, term, pair_t, hr, fs, fr, xt, gate_v, up_v, down_v,
    w_sem, o_sem, a_send, a_recv, s_send, s_recv, h_send, h_recv,
):
    dp = lax.axis_index("dp")
    hidden = lax.axis_index("hidden")
    z, y = dp // 4, dp % 4
    chip, core = hidden // 2, hidden % 2
    xx, zh = chip // 2, chip % 2
    other = 1 - core
    n = active_count(chip)
    z_pair = z + 1 - 2 * (z % 2)
    inner = jnp.logical_or(z == 1, z == 2)
    outer = jnp.logical_not(inner)
    y_opp, y_right, y_left = (y + 2) % 4, (y + 1) % 4, (y + 3) % 4
    partner = device(z, y, chip, other)
    right, left = device(z, y_right, chip, core), device(z, y_left, chip, core)

    def remote(src, dst, send, recv, target):
        return pltpu.make_async_remote_copy(
            src_ref=src, dst_ref=dst, send_sem=send, recv_sem=recv, device_id=target, device_id_type=MESH
        )

    loads = [
        pltpu.make_async_copy(src, dst, w_sem.at[k])
        for k, (src, dst) in enumerate(((wg_hbm, wg), (wu_hbm, wu), (wd_hbm, wd)))
    ]
    for load in loads:
        load.start()

    barrier = pltpu.get_barrier_semaphore()
    greeted = [partner, right, left]
    greeted += [device((z + k) % 4, y, chip, core) for k in (1, 2, 3)]
    greeted += [device(z, y, (chip + k) % CHIPS, core) for k in range(1, CHIPS)]
    for who in greeted:
        pl.semaphore_signal(barrier, inc=1, device_id=who, device_id_type=MESH)

    for array, ref in enumerate((x_ref, g_ref)):
        rows = []
        for u in range(UNITS):
            index = jnp.int32(0)
            for i in range(1, UNITS):
                index = jnp.where(lev[i] == UNITS - 1 - u, i, index)
            rows.append(ref[index].astype(F32))
        own[array * 32 : array * 32 + 16] = jnp.concatenate(rows[:2], 0).astype(BF16)
        own[array * 32 + 16 : array * 32 + 32] = jnp.concatenate(rows[2:], 0).astype(BF16)

    pl.semaphore_wait(barrier, len(greeted))

    pair_copy = remote(own, pair, a_send.at[0], a_recv.at[0], partner)
    pair_copy.start()
    pair_copy.wait()
    for u in range(0, UNITS, 2):
        rows = pl.ds(pl.multiple_of(core * 32 + u * 8, 16), 16)
        mine, theirs = own[rows].astype(F32), pair[rows].astype(F32)
        zero = jnp.where(core == 0, mine, theirs)
        one = jnp.where(core == 0, theirs, mine)
        xg[core, u, chip] = jnp.concatenate([zero[:8], one[:8]], 0).astype(BF16)
        xg[core, u + 1, chip] = jnp.concatenate([zero[8:], one[8:]], 0).astype(BF16)

    def block(c):
        return xg.at[core, :, c]

    far = 2 * xx + (1 - zh)
    spread = [remote(block(chip), block(chip), a_send.at[1], a_recv.at[1], device(z, y, far, core))]
    for k in (1, 2, 3):
        target = device(z, y, 2 * ((xx + k) % 4) + zh, core)
        spread.append(remote(block(chip), block(chip), a_send.at[1 + k], a_recv.at[1 + k], target))
    for copy in spread:
        copy.start()
    spread[0].wait_recv()
    for k in (1, 2, 3):
        target = device(z, y, 2 * ((xx + k) % 4) + zh, core)
        spread.append(remote(block(far), block(far), a_send.at[4 + k], a_recv.at[4 + k], target))
        spread[-1].start()
    for copy in spread[1:]:
        copy.wait_recv()
    for copy in spread:
        copy.wait_send()
    swap = remote(xg.at[core], xg.at[core], a_send.at[8], a_recv.at[8], partner)
    swap.start()
    swap.wait()
    for load in loads:
        load.wait()

    def piece(zd, q):
        first, width = SPANS[q]
        cols = pl.ds(pl.multiple_of(first + (zd % 2) * (width // 2), 128), width // 2)
        return pl.ds(y * 32 + (zd // 2) * 16, 16), cols

    def copy_of(u, q, kind):
        span = pl.ds(*SPANS[q])
        half_span = pl.ds(SPANS[q][0] // 2, SPANS[q][1] // 2)

        def part(ref, u, yy, half, count=16):
            return ref.at[u, :, pl.ds(yy * 32 + half * 16, count), span]

        if kind == 0:
            src, dst, to = part(pb, u, y_opp, 0), r1.at[u, 0, :, :, span], right
        elif kind == 1:
            src, dst, to = part(pb, u, y_opp, 1), r1.at[u, 1, :, :, span], left
        elif kind == 2:
            src, dst, to = part(pb, u, y_right, 1), r2.at[u, 0, :, pl.ds(16, 16), span], right
        elif kind == 3:
            src, dst, to = part(pb, u, y_left, 0), r2.at[u, 1, :, pl.ds(0, 16), span], left
        elif kind == 4:
            src, dst, to = r1.at[u, 0, :, :, span], r2.at[u, 0, :, pl.ds(0, 16), span], right
        elif kind == 5:
            src, dst, to = r1.at[u, 1, :, :, span], r2.at[u, 1, :, pl.ds(16, 16), span], left
        elif kind == 6:
            rows, cols = piece(z_pair, q)
            src = pf.at[u, :, rows, cols]
            dst, to = zr.at[u, 0, :, :, half_span], device(z_pair, y, chip, core)
        elif kind == 7:
            src, dst, to = zs.at[u, :, :, span], zx.at[u, :, :, span], device(z_pair, y, chip, core)
        elif kind in (8, 9):
            zd = 2 * (1 - z // 2) + kind - 8
            rows, cols = piece(zd, q)
            src = pf.at[u, :, rows, cols]
            dst, to = zr.at[u, 1, :, :, half_span], device(zd, y, chip, core)
        elif kind in (10, 11, 12):
            rows, cols = piece(z, q)
            src = dst = agb.at[u, :, rows, cols]
            to = device((z + kind - 9) % 4, y, chip, core)
        elif kind in (13, 14):
            src = dst = part(agb, u, y, 0, 32)
            to = (right, left)[kind - 13]
        elif kind == 15:
            src = dst = part(agb, u, y_left, 0)
            to = right
        elif kind == 16:
            src = dst = part(agb, u, y_right, 1)
            to = left
        elif kind == 17:
            src = dst = pb.at[u, :, :, span]
            to = device(z, y, 2 * lender(u, q) + zh, core)
        else:
            src = dst = agb.at[u, :, :, span]
            to = device(z, y, zh, core)
        return remote(src, dst, s_send.at[u, q, kind], s_recv.at[u, q, 8 if kind == 9 else kind], to)

    def lender(u, q):
        where = jnp.int32(1)
        for (unit, span), x_to in LENT.items():
            if span == q:
                where = jnp.where(u == unit, x_to, where)
        return where

    def lent(u, q):
        found = jnp.bool_(False)
        for unit, span in LENT:
            if span == q:
                found = jnp.logical_or(found, u == unit)
        return jnp.logical_and(found, jnp.logical_and(xx == 0, u < n))

    def taken(u, q):
        found = jnp.bool_(False)
        for (unit, span), x_to in LENT.items():
            if span == q:
                found = jnp.logical_or(found, jnp.logical_and(u == unit, xx == x_to))
        return jnp.logical_and(found, u < active_count(zh))

    def pair_term(u):
        return remote(term.at[u, other], pair_t.at[u], h_send.at[u, 7], h_recv.at[u, 8], partner)

    def chip_term(u, k):
        target = (chip + k) % CHIPS
        return remote(
            term.at[u, core, pl.ds(target * 16, 16), :], hr.at[u, chip],
            h_send.at[u, k - 1], h_recv.at[u, chip], device(z, y, target, core),
        )

    def dots(u, q):
        def tile(i, _):
            cols = pl.ds(pl.multiple_of(i * TILE, TILE), TILE)
            rows_x = xg[0, u].reshape(TOK, FEAT)
            rows_g = xg[1, u].reshape(TOK, FEAT)
            values = (
                jnp.dot(rows_x, wg[:, cols], preferred_element_type=F32),
                jnp.dot(rows_x, wu[:, cols], preferred_element_type=F32),
                lax.dot_general(rows_g, wd[cols, :], NT, preferred_element_type=F32),
            )
            for k, value in enumerate(values):
                pf[u, k, :, cols] = value
                pb[u, k, :, cols] = value.astype(BF16)
            return 0

        first, width = SPANS[q]

        @pl.when(u < n)
        def _():
            lax.fori_loop(first // TILE, (first + width) // TILE, tile, 0)

        @pl.when(lent(u, q))
        def _():
            copy_of(u, q, 17).start()

        @pl.when(taken(u, q))
        def _():
            copy_of(u, q, 17).wait_recv()
            for k in range(3):
                pf[u, k, :, first : first + width] = pb[u, k, :, first : first + width].astype(F32)

        @pl.when(jnp.logical_not(lent(u, q)))
        def _():
            for kind in range(4):
                copy_of(u, q, kind).start()

    def accumulate(u, q):
        span = pl.ds(*SPANS[q])
        for side, (kind, yy) in enumerate(((0, y_right), (1, y_left))):
            copy_of(u, q, kind).wait_recv()
            rows = pl.ds(yy * 32 + side * 16, 16)
            for k in range(3):
                r1[u, side, k, :, span] = (r1[u, side, k, :, span].astype(F32) + pf[u, k, rows, span]).astype(BF16)
            copy_of(u, q, kind + 4).start()

    def sum_y(u, q):
        span = pl.ds(*SPANS[q])
        for kind in (2, 3, 4, 5):
            copy_of(u, q, kind).wait_recv()
        rows = pl.ds(y * 32, 32)
        for k in range(3):
            pf[u, k, rows, span] += r2[u, 0, k, :, span].astype(F32) + r2[u, 1, k, :, span].astype(F32)
        copy_of(u, q, 6).start()

        @pl.when(outer)
        def _():
            across = pl.ds(y * 32 + (1 - z // 2) * 16, 16)
            for k in range(3):
                zs[u, k, :, span] = pf[u, k, across, span].astype(BF16)
            copy_of(u, q, 7).start()

    def sum_pair(u, q):
        @pl.when(inner)
        def _():
            span = pl.ds(*SPANS[q])
            across = pl.ds(y * 32 + (1 - z // 2) * 16, 16)
            copy_of(u, q, 7).wait_recv()
            for k in range(3):
                pf[u, k, across, span] += zx[u, k, :, span].astype(F32)
            for kind in (8, 9):
                copy_of(u, q, kind).start()

    def units(u, q):
        for kind in (6, 8):
            copy_of(u, q, kind).wait_recv()
        rows, cols = piece(z, q)
        half_span = pl.ds(SPANS[q][0] // 2, SPANS[q][1] // 2)
        gate, up, grad = (
            pf[u, k, rows, cols] + (zr[u, 0, k, :, half_span] + zr[u, 1, k, :, half_span]) for k in range(3)
        )
        s = jax.nn.sigmoid(gate)
        agb[u, 0, rows, cols] = (gate * s * up).astype(BF16)
        agb[u, 1, rows, cols] = (grad * up * s * (1.0 + gate * (1.0 - s))).astype(BF16)
        agb[u, 2, rows, cols] = (grad * gate * s).astype(BF16)
        for kind in (10, 11, 12):
            copy_of(u, q, kind).start()

    def spread_y(u, q):
        for kind in (10, 11, 12):
            copy_of(u, q, kind).wait_recv()
        for kind in (13, 14):
            copy_of(u, q, kind).start()

    def forward_y(u, q):
        for kind in (13, 14):
            copy_of(u, q, kind).wait_recv()
            copy_of(u, q, kind + 2).start()

    def add_term(u, q):
        first, width = SPANS[q]
        span = slice(first, first + width)
        for half in range(2):
            feats = slice(half * TILE, half * TILE + TILE)
            term[u, half] += lax.dot_general(
                agb[u, 1, :, span], wg[feats, span], NT, preferred_element_type=F32
            ) + lax.dot_general(agb[u, 2, :, span], wu[feats, span], NT, preferred_element_type=F32)

    def back(u, q):
        for kind in (15, 16):
            copy_of(u, q, kind).wait_recv()

        @pl.when(taken(u, q))
        def _():
            copy_of(u, q, 18).start()

        @pl.when(jnp.logical_not(taken(u, q)))
        def _():
            add_term(u, q)

    def finish(u):
        pair_term(u).start()

    def send_terms(u):
        pair_term(u).wait_recv()
        term[u, core] += pair_t[u]
        for k in range(1, CHIPS):
            chip_term(u, k).start()

    stages = (dots, accumulate, sum_y, sum_pair, units, spread_y, forward_y, back)
    spans = len(SPANS)
    for u in range(UNITS):
        term[u] = jnp.zeros((2, TOK, TILE), F32)

    def unit_at(turn):
        u = jnp.int32(0)
        for index, (first, second) in enumerate(zip(ORDER, ORDER_LENDER)):
            u = jnp.where(turn == index, jnp.where(xx == 0, second, first), u)
        return u

    def step(t, _):
        for q_now in range(spans):
            for lag in reversed(range(len(stages))):
                q = (q_now - LAGS[lag]) % spans
                turn = t + (q_now - LAGS[lag]) // spans
                u = unit_at(turn)
                here = jnp.logical_and(turn >= 0, turn < UNITS)
                mine = jnp.logical_or(u < n, taken(u, q))
                if lag > 0:
                    mine = jnp.logical_and(mine, jnp.logical_not(lent(u, q)))

                @pl.when(jnp.logical_and(here, mine))
                def _(u=u, q=q, lag=lag):
                    stages[lag](u, q)

                if lag == len(stages) - 1 and q == spans - 1:

                    @pl.when(jnp.logical_and(here, jnp.logical_and(u < n, jnp.logical_not(any_lent(u)))))
                    def _(u=u):
                        finish(u)

        return 0

    def any_lent(u):
        found = lent(u, 0)
        for q in range(1, spans):
            found = jnp.logical_or(found, lent(u, q))
        return found

    lax.fori_loop(0, UNITS + (LAGS[-1] + spans - 1) // spans, step, 0)

    for unit in sorted({unit for unit, _ in LENT}):
        for q in range(spans):
            if (unit, q) in LENT:

                @pl.when(lent(unit, q))
                def _(unit=unit, q=q):
                    copy_of(unit, q, 18).wait_recv()
                    add_term(unit, q)

        @pl.when(any_lent(unit))
        def _(unit=unit):
            finish(unit)

    def spread_terms(u, _):
        send_terms(u)
        return 0

    lax.fori_loop(0, n, spread_terms, 0)

    def clear(u, _):
        for q in range(spans):

            @pl.when(taken(u, q))
            def _(q=q):
                copy_of(u, q, 18).wait_send()
                for kind in range(10, 17):
                    copy_of(u, q, kind).wait_send()

        agb[u] = jnp.zeros((3, TOK, WIDTH), BF16)
        return 0

    lax.fori_loop(n, UNITS, clear, 0)

    def store(i, k):
        cols = pl.ds(pl.multiple_of(i * TILE, TILE), TILE)
        if k == 2:
            return pltpu.make_async_copy(down_v.at[cols, :], down_hbm.at[cols, :], o_sem.at[k, i])
        src, dst = ((gate_v, gate_hbm), (up_v, up_hbm))[k]
        return pltpu.make_async_copy(src.at[:, cols], dst.at[:, cols], o_sem.at[k, i])

    xt[...] = xg[0].reshape(UNITS * TOK, FEAT).T

    def weights(i, _):
        cols = pl.ds(pl.multiple_of(i * TILE, TILE), TILE)
        act, dgate, dup = (agb[:, k, :, cols].reshape(UNITS * TOK, TILE) for k in range(3))
        gate_v[:, cols] = jnp.dot(xt[...], dgate, preferred_element_type=F32).astype(BF16)
        store(i, 0).start()
        up_v[:, cols] = jnp.dot(xt[...], dup, preferred_element_type=F32).astype(BF16)
        store(i, 1).start()
        down_v[cols, :] = lax.dot_general(
            act, xg[1].reshape(UNITS * TOK, FEAT), (((0,), (0,)), ((), ())), preferred_element_type=F32
        ).astype(BF16)
        store(i, 2).start()
        return 0

    lax.fori_loop(0, WIDTH // TILE, weights, 0)

    for u in range(UNITS):
        fs[u] = jnp.zeros((16, TILE), F32)

        def add(j, _, u=u):
            @pl.when(j == chip)
            def _():
                fs[u] += term[u, core, pl.ds(chip * 16, 16), :]

            @pl.when(j != chip)
            def _():
                remote(
                    hr.at[u, j], hr.at[u, j], h_send.at[u, 0], h_recv.at[u, j], device(z, y, j, core)
                ).wait_recv()
                fs[u] += hr[u, j]

            return 0

        lax.fori_loop(0, (8, 4, 2, 1)[u], add, 0)

    last = remote(
        fs.at[:, pl.ds(pl.multiple_of(other * 8, 8), 8), :], fr, a_send.at[9], a_recv.at[9], partner
    )
    last.start()
    last.wait()
    here = pl.ds(pl.multiple_of(core * TILE, TILE), TILE)
    there = pl.ds(pl.multiple_of(other * TILE, TILE), TILE)
    mine = pl.ds(pl.multiple_of(core * 8, 8), 8)
    for b in range(UNITS):
        u = UNITS - 1 - lev[b]
        in_grad[b, :, here] = fs[u, mine, :].astype(BF16)
        in_grad[b, :, there] = fr[u].astype(BF16)

    def drain(u, _):
        pair_term(u).wait_send()
        for k in range(1, CHIPS):
            chip_term(u, k).wait_send()
        return 0

    lax.fori_loop(0, n, drain, 0)

    def drain_sums(u, _):
        for q in range(spans):

            @pl.when(lent(u, q))
            def _(q=q):
                copy_of(u, q, 17).wait_send()

            @pl.when(jnp.logical_or(taken(u, q), jnp.logical_and(u < n, jnp.logical_not(lent(u, q)))))
            def _(q=q):
                for kind in range(7):
                    copy_of(u, q, kind).wait_send()

                @pl.when(outer)
                def _():
                    copy_of(u, q, 7).wait_send()

                @pl.when(inner)
                def _():
                    for kind in (8, 9):
                        copy_of(u, q, kind).wait_send()

            @pl.when(jnp.logical_and(u < n, jnp.logical_not(lent(u, q))))
            def _(q=q):
                for kind in range(10, 17):
                    copy_of(u, q, kind).wait_send()

        return 0

    lax.fori_loop(0, UNITS, drain_sums, 0)
    for i in range(WIDTH // TILE):
        for k in range(3):
            store(i, k).wait()


def exchange(levels, activations, out_grad, w_gate, w_up, w_down):
    vmem = pl.BlockSpec(memory_space=pltpu.VMEM)
    hbm = pl.BlockSpec(memory_space=pl.ANY)
    dma = pltpu.SemaphoreType.DMA
    return pl.pallas_call(
        kernel,
        out_shape=[
            jax.ShapeDtypeStruct(activations.shape, BF16),
            jax.ShapeDtypeStruct((FEAT, WIDTH), BF16),
            jax.ShapeDtypeStruct((FEAT, WIDTH), BF16),
            jax.ShapeDtypeStruct((WIDTH, FEAT), BF16),
        ],
        in_specs=[pl.BlockSpec(memory_space=pltpu.SMEM), vmem, vmem, hbm, hbm, hbm],
        out_specs=[vmem, hbm, hbm, hbm],
        scratch_shapes=[
            pltpu.VMEM((FEAT, WIDTH), BF16),
            pltpu.VMEM((FEAT, WIDTH), BF16),
            pltpu.VMEM((WIDTH, FEAT), BF16),
            pltpu.VMEM((64, FEAT), BF16),
            pltpu.VMEM((64, FEAT), BF16),
            pltpu.VMEM((2, UNITS, CHIPS, 16, FEAT), BF16),
            pltpu.VMEM((UNITS, 3, TOK, WIDTH), F32),
            pltpu.VMEM((UNITS, 3, TOK, WIDTH), BF16),
            pltpu.VMEM((UNITS, 2, 3, 16, WIDTH), BF16),
            pltpu.VMEM((UNITS, 2, 3, 32, WIDTH), BF16),
            pltpu.VMEM((UNITS, 2, 3, 16, WIDTH // 2), F32),
            pltpu.VMEM((UNITS, 3, 16, WIDTH), BF16),
            pltpu.VMEM((UNITS, 3, 16, WIDTH), BF16),
            pltpu.VMEM((UNITS, 3, TOK, WIDTH), BF16),
            pltpu.VMEM((UNITS, 2, TOK, TILE), F32),
            pltpu.VMEM((UNITS, TOK, TILE), F32),
            pltpu.VMEM((UNITS, CHIPS, 16, TILE), F32),
            pltpu.VMEM((UNITS, 16, TILE), F32),
            pltpu.VMEM((UNITS, 8, TILE), F32),
            pltpu.VMEM((FEAT, UNITS * TOK), BF16),
            pltpu.VMEM((FEAT, WIDTH), BF16),
            pltpu.VMEM((FEAT, WIDTH), BF16),
            pltpu.VMEM((WIDTH, FEAT), BF16),
            dma((3,)),
            dma((3, WIDTH // TILE)),
            dma((10,)),
            dma((10,)),
            dma((UNITS, len(SPANS), 19)),
            dma((UNITS, len(SPANS), 19)),
            dma((UNITS, 8)),
            dma((UNITS, 9)),
        ],
        compiler_params=pltpu.CompilerParams(
            collective_id=0, has_side_effects=True, vmem_limit_bytes=56 * 1024 * 1024
        ),
    )(levels, activations, out_grad, w_gate, w_up, w_down)


def body(activations, out_grad, w_gate, w_up, w_down, levels):
    return exchange(levels, activations, out_grad, w_gate, w_up, w_down)


def solution(mesh):
    placed = (
        P(None, "hidden", "dp"),
        P(None, "hidden", "dp"),
        P("dp", "hidden"),
        P("dp", "hidden"),
        P("hidden", "dp"),
        P(),
    )
    return jax.shard_map(
        body,
        mesh=mesh,
        in_specs=placed,
        out_specs=(
            P(None, "hidden", "dp"),
            P("dp", "hidden"),
            P("dp", "hidden"),
            P("hidden", "dp"),
        ),
        check_vma=False,
    )
```

```python
import jax
import jax.numpy as jnp
from jax import lax
from jax.experimental import pallas as pl
from jax.experimental.pallas import tpu as pltpu
from jax.sharding import PartitionSpec as P

MESH = pl.DeviceIdType.MESH
BF16 = jnp.bfloat16
F32 = jnp.float32

UNITS = 4
TOK = 128
FEAT = 512
WIDTH = 1792
TILE = 256
CHIPS = 8
SPANS = ((0, 256), (256, 256), (512, 256), (768, 256), (1024, 256), (1280, 256), (1536, 256))
LENT = {(3, 0): 1, (3, 1): 3, (3, 2): 2, (3, 3): 1, (3, 4): 3, (3, 5): 2, (3, 6): 3, (2, 0): 1, (2, 1): 3}
NT = (((1,), (1,)), ((), ()))
COPIES = 4
ORDER_LENDER = (3, 2, 1, 0)
ORDER = (0, 3, 2, 1)
LAGS = (0, 3, 6, 9, 12, 15, 18, 21)


def device(z, y, chip, core):
    return (z * 4 + y, chip * 2 + core)


def active_count(chip):
    return 1 + (chip < 4).astype(jnp.int32) + (chip < 2) + (chip < 1)


def kernel(
    lev, x_ref, g_ref, wg_hbm, wu_hbm, wd_hbm,
    in_grad, gate_hbm, up_hbm, down_hbm,
    wg, wu, wd, own, pair, xg, pf, pb, r1, r2, zr, zs, zx, agb, term, pair_t, hr, fs, fr, xt, gate_v, up_v, down_v,
    w_sem, o_sem, a_send, a_recv, s_send, s_recv, h_send, h_recv,
):
    dp = lax.axis_index("dp")
    hidden = lax.axis_index("hidden")
    z, y = dp // 4, dp % 4
    chip, core = hidden // 2, hidden % 2
    xx, zh = chip // 2, chip % 2
    other = 1 - core
    n = active_count(chip)
    z_pair = z + 1 - 2 * (z % 2)
    inner = jnp.logical_or(z == 1, z == 2)
    outer = jnp.logical_not(inner)
    y_opp, y_right, y_left = (y + 2) % 4, (y + 1) % 4, (y + 3) % 4
    partner = device(z, y, chip, other)
    right, left = device(z, y_right, chip, core), device(z, y_left, chip, core)

    def remote(src, dst, send, recv, target):
        return pltpu.make_async_remote_copy(
            src_ref=src, dst_ref=dst, send_sem=send, recv_sem=recv, device_id=target, device_id_type=MESH
        )

    loads = [
        pltpu.make_async_copy(src, dst, w_sem.at[k])
        for k, (src, dst) in enumerate(((wg_hbm, wg), (wu_hbm, wu), (wd_hbm, wd)))
    ]
    for load in loads:
        load.start()

    barrier = pltpu.get_barrier_semaphore()
    greeted = [partner, right, left]
    greeted += [device((z + k) % 4, y, chip, core) for k in (1, 2, 3)]
    greeted += [device(z, y, (chip + k) % CHIPS, core) for k in range(1, CHIPS)]
    for who in greeted:
        pl.semaphore_signal(barrier, inc=1, device_id=who, device_id_type=MESH)

    for array, ref in enumerate((x_ref, g_ref)):
        rows = []
        for u in range(UNITS):
            index = jnp.int32(0)
            for i in range(1, UNITS):
                index = jnp.where(lev[i] == UNITS - 1 - u, i, index)
            rows.append(ref[index].astype(F32))
        own[array * 32 : array * 32 + 16] = jnp.concatenate(rows[:2], 0).astype(BF16)
        own[array * 32 + 16 : array * 32 + 32] = jnp.concatenate(rows[2:], 0).astype(BF16)

    pl.semaphore_wait(barrier, len(greeted))

    far = 2 * xx + (1 - zh)

    def pair_copy(part):
        rows = pl.ds(pl.multiple_of(other * 32 + part * 16, 16), 16)
        return remote(own.at[rows], pair.at[rows], a_send.at[part, 0], a_recv.at[part, 0], partner)

    def block(part, c):
        return xg.at[core, pl.ds(part * 2, 2), c]

    def gather_z(part):
        ref = block(part, chip)
        return remote(ref, ref, a_send.at[part, 1], a_recv.at[part, 1], device(z, y, far, core))

    def gather_x(part, c, k, slot):
        ref = block(part, c)
        target = device(z, y, 2 * ((xx + k) % 4) + zh, core)
        return remote(ref, ref, a_send.at[part, slot], a_recv.at[part, slot], target)

    def swap(part):
        ref = xg.at[core, pl.ds(part * 2, 2)]
        return remote(ref, ref, a_send.at[part, 8], a_recv.at[part, 8], partner)

    for part in (1, 0):
        pair_copy(part).start()
    for part in (1, 0):
        pair_copy(part).wait_recv()
        rows = pl.ds(pl.multiple_of(core * 32 + part * 16, 16), 16)
        mine, theirs = own[rows].astype(F32), pair[rows].astype(F32)
        zero = jnp.where(core == 0, mine, theirs)
        one = jnp.where(core == 0, theirs, mine)
        xg[core, 2 * part, chip] = jnp.concatenate([zero[:8], one[:8]], 0).astype(BF16)
        xg[core, 2 * part + 1, chip] = jnp.concatenate([zero[8:], one[8:]], 0).astype(BF16)
        gather_z(part).start()
        for k in (1, 2, 3):
            gather_x(part, chip, k, 1 + k).start()
    for part in (1, 0):
        gather_z(part).wait_recv()
        for k in (1, 2, 3):
            gather_x(part, far, k, 4 + k).start()

    def start_swap(part):
        for k in (1, 2, 3):
            gather_x(part, chip, k, 1 + k).wait_recv()
            gather_x(part, far, k, 4 + k).wait_recv()
        swap(part).start()

    start_swap(1)

    @pl.when(xx != 0)
    def _():
        start_swap(0)
        swap(0).wait_recv()

    swap(1).wait_recv()
    for load in loads:
        load.wait()

    def piece(zd, q):
        first, width = SPANS[q]
        cols = pl.ds(pl.multiple_of(first + (zd % 2) * (width // 2), 128), width // 2)
        return pl.ds(y * 32 + (zd // 2) * 16, 16), cols

    def copy_of(u, q, kind):
        span = pl.ds(*SPANS[q])
        half_span = pl.ds(SPANS[q][0] // 2, SPANS[q][1] // 2)

        def part(ref, u, yy, half, count=16):
            return ref.at[u, :, pl.ds(yy * 32 + half * 16, count), span]

        if kind == 0:
            src, dst, to = part(pb, u, y_opp, 0), r1.at[u, 0, :, :, span], right
        elif kind == 1:
            src, dst, to = part(pb, u, y_opp, 1), r1.at[u, 1, :, :, span], left
        elif kind == 2:
            src, dst, to = part(pb, u, y_right, 1), r2.at[u, 0, :, pl.ds(16, 16), span], right
        elif kind == 3:
            src, dst, to = part(pb, u, y_left, 0), r2.at[u, 1, :, pl.ds(0, 16), span], left
        elif kind == 4:
            src, dst, to = r1.at[u, 0, :, :, span], r2.at[u, 0, :, pl.ds(0, 16), span], right
        elif kind == 5:
            src, dst, to = r1.at[u, 1, :, :, span], r2.at[u, 1, :, pl.ds(16, 16), span], left
        elif kind == 6:
            rows, cols = piece(z_pair, q)
            src = pf.at[u, :, rows, cols]
            dst, to = zr.at[u, 0, :, :, half_span], device(z_pair, y, chip, core)
        elif kind == 7:
            src, dst, to = zs.at[u, :, :, span], zx.at[u, :, :, span], device(z_pair, y, chip, core)
        elif kind in (8, 9):
            zd = 2 * (1 - z // 2) + kind - 8
            rows, cols = piece(zd, q)
            src = pf.at[u, :, rows, cols]
            dst, to = zr.at[u, 1, :, :, half_span], device(zd, y, chip, core)
        elif kind in (10, 11, 12):
            rows, cols = piece(z, q)
            src = dst = agb.at[u, :, rows, cols]
            to = device((z + kind - 9) % 4, y, chip, core)
        elif kind in (13, 14):
            src = dst = part(agb, u, y, 0, 32)
            to = (right, left)[kind - 13]
        elif kind == 15:
            src = dst = part(agb, u, y_left, 0)
            to = right
        elif kind == 16:
            src = dst = part(agb, u, y_right, 1)
            to = left
        elif kind == 17:
            src = dst = pb.at[u, :, :, span]
            to = device(z, y, 2 * lender(u, q) + zh, core)
        else:
            src = dst = agb.at[u, :, :, span]
            to = device(z, y, zh, core)
        return remote(src, dst, s_send.at[u, q, kind], s_recv.at[u, q, 8 if kind == 9 else kind], to)

    def lender(u, q):
        where = jnp.int32(1)
        for (unit, span), x_to in LENT.items():
            if span == q:
                where = jnp.where(u == unit, x_to, where)
        return where

    def lent(u, q):
        found = jnp.bool_(False)
        for unit, span in LENT:
            if span == q:
                found = jnp.logical_or(found, u == unit)
        return jnp.logical_and(found, jnp.logical_and(xx == 0, u < n))

    def taken(u, q):
        found = jnp.bool_(False)
        for (unit, span), x_to in LENT.items():
            if span == q:
                found = jnp.logical_or(found, jnp.logical_and(u == unit, xx == x_to))
        return jnp.logical_and(found, u < active_count(zh))

    def pair_term(u):
        return remote(term.at[u, other], pair_t.at[u], h_send.at[u, 7], h_recv.at[u, 8], partner)

    def chip_term(u, k):
        target = (chip + k) % CHIPS
        return remote(
            term.at[u, core, pl.ds(target * 16, 16), :], hr.at[u, chip],
            h_send.at[u, k - 1], h_recv.at[u, chip], device(z, y, target, core),
        )

    def dots(u, q):
        def tile(i, _):
            cols = pl.ds(pl.multiple_of(i * TILE, TILE), TILE)
            rows_x = xg[0, u].reshape(TOK, FEAT)
            rows_g = xg[1, u].reshape(TOK, FEAT)
            values = (
                jnp.dot(rows_x, wg[:, cols], preferred_element_type=F32),
                jnp.dot(rows_x, wu[:, cols], preferred_element_type=F32),
                lax.dot_general(rows_g, wd[cols, :], NT, preferred_element_type=F32),
            )
            for k, value in enumerate(values):
                pf[u, k, :, cols] = value
                pb[u, k, :, cols] = value.astype(BF16)
            return 0

        first, width = SPANS[q]
        if q == 0:

            @pl.when(jnp.logical_and(xx == 0, u == UNITS - 2))
            def _():
                start_swap(0)

            @pl.when(jnp.logical_and(xx == 0, u == 1))
            def _():
                swap(0).wait_recv()

        @pl.when(u < n)
        def _():
            lax.fori_loop(first // TILE, (first + width) // TILE, tile, 0)

        @pl.when(lent(u, q))
        def _():
            copy_of(u, q, 17).start()

        @pl.when(taken(u, q))
        def _():
            copy_of(u, q, 17).wait_recv()
            for k in range(3):
                pf[u, k, :, first : first + width] = pb[u, k, :, first : first + width].astype(F32)

        @pl.when(jnp.logical_not(lent(u, q)))
        def _():
            for kind in range(4):
                copy_of(u, q, kind).start()

    def accumulate(u, q):
        span = pl.ds(*SPANS[q])
        for side, (kind, yy) in enumerate(((0, y_right), (1, y_left))):
            copy_of(u, q, kind).wait_recv()
            rows = pl.ds(yy * 32 + side * 16, 16)
            for k in range(3):
                r1[u, side, k, :, span] = (r1[u, side, k, :, span].astype(F32) + pf[u, k, rows, span]).astype(BF16)
            copy_of(u, q, kind + 4).start()

    def sum_y(u, q):
        span = pl.ds(*SPANS[q])
        for kind in (2, 3, 4, 5):
            copy_of(u, q, kind).wait_recv()
        rows = pl.ds(y * 32, 32)
        for k in range(3):
            pf[u, k, rows, span] += r2[u, 0, k, :, span].astype(F32) + r2[u, 1, k, :, span].astype(F32)
        copy_of(u, q, 6).start()

        @pl.when(outer)
        def _():
            across = pl.ds(y * 32 + (1 - z // 2) * 16, 16)
            for k in range(3):
                zs[u, k, :, span] = pf[u, k, across, span].astype(BF16)
            copy_of(u, q, 7).start()

    def sum_pair(u, q):
        @pl.when(inner)
        def _():
            span = pl.ds(*SPANS[q])
            across = pl.ds(y * 32 + (1 - z // 2) * 16, 16)
            copy_of(u, q, 7).wait_recv()
            for k in range(3):
                pf[u, k, across, span] += zx[u, k, :, span].astype(F32)
            for kind in (8, 9):
                copy_of(u, q, kind).start()

    def units(u, q):
        for kind in (6, 8):
            copy_of(u, q, kind).wait_recv()
        rows, cols = piece(z, q)
        half_span = pl.ds(SPANS[q][0] // 2, SPANS[q][1] // 2)
        gate, up, grad = (
            pf[u, k, rows, cols] + (zr[u, 0, k, :, half_span] + zr[u, 1, k, :, half_span]) for k in range(3)
        )
        s = jax.nn.sigmoid(gate)
        agb[u, 0, rows, cols] = (gate * s * up).astype(BF16)
        agb[u, 1, rows, cols] = (grad * up * s * (1.0 + gate * (1.0 - s))).astype(BF16)
        agb[u, 2, rows, cols] = (grad * gate * s).astype(BF16)
        for kind in (10, 11, 12):
            copy_of(u, q, kind).start()

    def spread_y(u, q):
        for kind in (10, 11, 12):
            copy_of(u, q, kind).wait_recv()
        for kind in (13, 14):
            copy_of(u, q, kind).start()

    def forward_y(u, q):
        for kind in (13, 14):
            copy_of(u, q, kind).wait_recv()
            copy_of(u, q, kind + 2).start()

    def add_term(u, q):
        first, width = SPANS[q]
        span = slice(first, first + width)
        for half in range(2):
            feats = slice(half * TILE, half * TILE + TILE)
            term[u, half] += lax.dot_general(
                agb[u, 1, :, span], wg[feats, span], NT, preferred_element_type=F32
            ) + lax.dot_general(agb[u, 2, :, span], wu[feats, span], NT, preferred_element_type=F32)

    def back(u, q):
        for kind in (15, 16):
            copy_of(u, q, kind).wait_recv()

        @pl.when(taken(u, q))
        def _():
            copy_of(u, q, 18).start()

        @pl.when(jnp.logical_not(taken(u, q)))
        def _():
            add_term(u, q)

    def finish(u):
        pair_term(u).start()

    def send_terms(u):
        pair_term(u).wait_recv()
        term[u, core] += pair_t[u]
        for k in range(1, CHIPS):
            chip_term(u, k).start()

    stages = (dots, accumulate, sum_y, sum_pair, units, spread_y, forward_y, back)
    spans = len(SPANS)
    for u in range(UNITS):
        term[u] = jnp.zeros((2, TOK, TILE), F32)

    def unit_at(turn):
        u = jnp.int32(0)
        for index, (first, second) in enumerate(zip(ORDER, ORDER_LENDER)):
            u = jnp.where(turn == index, jnp.where(xx == 0, second, first), u)
        return u

    def step(t, _):
        for q_now in range(spans):
            for lag in reversed(range(len(stages))):
                q = (q_now - LAGS[lag]) % spans
                turn = t + (q_now - LAGS[lag]) // spans
                u = unit_at(turn)
                here = jnp.logical_and(turn >= 0, turn < UNITS)
                mine = jnp.logical_or(u < n, taken(u, q))
                if lag > 0:
                    mine = jnp.logical_and(mine, jnp.logical_not(lent(u, q)))

                @pl.when(jnp.logical_and(here, mine))
                def _(u=u, q=q, lag=lag):
                    stages[lag](u, q)

                if lag == len(stages) - 1 and q == spans - 1:

                    @pl.when(jnp.logical_and(here, jnp.logical_and(u < n, jnp.logical_not(any_lent(u)))))
                    def _(u=u):
                        finish(u)

        return 0

    def any_lent(u):
        found = lent(u, 0)
        for q in range(1, spans):
            found = jnp.logical_or(found, lent(u, q))
        return found

    lax.fori_loop(0, UNITS + (LAGS[-1] + spans - 1) // spans, step, 0)

    for unit in sorted({unit for unit, _ in LENT}):
        for q in range(spans):
            if (unit, q) in LENT:

                @pl.when(lent(unit, q))
                def _(unit=unit, q=q):
                    copy_of(unit, q, 18).wait_recv()
                    add_term(unit, q)

        @pl.when(any_lent(unit))
        def _(unit=unit):
            finish(unit)

    def spread_terms(u, _):
        send_terms(u)
        return 0

    lax.fori_loop(0, n, spread_terms, 0)

    def clear(u, _):
        for q in range(spans):

            @pl.when(taken(u, q))
            def _(q=q):
                copy_of(u, q, 18).wait_send()
                for kind in range(10, 17):
                    copy_of(u, q, kind).wait_send()

        agb[u] = jnp.zeros((3, TOK, WIDTH), BF16)
        return 0

    lax.fori_loop(n, UNITS, clear, 0)

    def store(i, k):
        cols = pl.ds(pl.multiple_of(i * TILE, TILE), TILE)
        if k == 2:
            return pltpu.make_async_copy(down_v.at[cols, :], down_hbm.at[cols, :], o_sem.at[k, i])
        src, dst = ((gate_v, gate_hbm), (up_v, up_hbm))[k]
        return pltpu.make_async_copy(src.at[:, cols], dst.at[:, cols], o_sem.at[k, i])

    xt[...] = xg[0].reshape(UNITS * TOK, FEAT).T

    def weights(i, _):
        cols = pl.ds(pl.multiple_of(i * TILE, TILE), TILE)
        act, dgate, dup = (agb[:, k, :, cols].reshape(UNITS * TOK, TILE) for k in range(3))
        gate_v[:, cols] = jnp.dot(xt[...], dgate, preferred_element_type=F32).astype(BF16)
        store(i, 0).start()
        up_v[:, cols] = jnp.dot(xt[...], dup, preferred_element_type=F32).astype(BF16)
        store(i, 1).start()
        down_v[cols, :] = lax.dot_general(
            act, xg[1].reshape(UNITS * TOK, FEAT), (((0,), (0,)), ((), ())), preferred_element_type=F32
        ).astype(BF16)
        store(i, 2).start()
        return 0

    lax.fori_loop(0, WIDTH // TILE, weights, 0)

    for u in range(UNITS):
        fs[u] = jnp.zeros((16, TILE), F32)

        def add(j, _, u=u):
            @pl.when(j == chip)
            def _():
                fs[u] += term[u, core, pl.ds(chip * 16, 16), :]

            @pl.when(j != chip)
            def _():
                remote(
                    hr.at[u, j], hr.at[u, j], h_send.at[u, 0], h_recv.at[u, j], device(z, y, j, core)
                ).wait_recv()
                fs[u] += hr[u, j]

            return 0

        lax.fori_loop(0, (8, 4, 2, 1)[u], add, 0)

    last = remote(
        fs.at[:, pl.ds(pl.multiple_of(other * 8, 8), 8), :], fr, a_send.at[0, 9], a_recv.at[0, 9], partner
    )
    last.start()
    last.wait()
    here = pl.ds(pl.multiple_of(core * TILE, TILE), TILE)
    there = pl.ds(pl.multiple_of(other * TILE, TILE), TILE)
    mine = pl.ds(pl.multiple_of(core * 8, 8), 8)
    for b in range(UNITS):
        u = UNITS - 1 - lev[b]
        in_grad[b, :, here] = fs[u, mine, :].astype(BF16)
        in_grad[b, :, there] = fr[u].astype(BF16)

    def drain(u, _):
        pair_term(u).wait_send()
        for k in range(1, CHIPS):
            chip_term(u, k).wait_send()
        return 0

    lax.fori_loop(0, n, drain, 0)
    for part in (1, 0):
        pair_copy(part).wait_send()
        gather_z(part).wait_send()
        for k in (1, 2, 3):
            gather_x(part, chip, k, 1 + k).wait_send()
            gather_x(part, far, k, 4 + k).wait_send()
        swap(part).wait_send()

    def drain_sums(u, _):
        for q in range(spans):

            @pl.when(lent(u, q))
            def _(q=q):
                copy_of(u, q, 17).wait_send()

            @pl.when(jnp.logical_or(taken(u, q), jnp.logical_and(u < n, jnp.logical_not(lent(u, q)))))
            def _(q=q):
                for kind in range(7):
                    copy_of(u, q, kind).wait_send()

                @pl.when(outer)
                def _():
                    copy_of(u, q, 7).wait_send()

                @pl.when(inner)
                def _():
                    for kind in (8, 9):
                        copy_of(u, q, kind).wait_send()

            @pl.when(jnp.logical_and(u < n, jnp.logical_not(lent(u, q))))
            def _(q=q):
                for kind in range(10, 17):
                    copy_of(u, q, kind).wait_send()

        return 0

    lax.fori_loop(0, UNITS, drain_sums, 0)
    for i in range(WIDTH // TILE):
        for k in range(3):
            store(i, k).wait()


def exchange(levels, activations, out_grad, w_gate, w_up, w_down):
    vmem = pl.BlockSpec(memory_space=pltpu.VMEM)
    hbm = pl.BlockSpec(memory_space=pl.ANY)
    dma = pltpu.SemaphoreType.DMA
    return pl.pallas_call(
        kernel,
        out_shape=[
            jax.ShapeDtypeStruct(activations.shape, BF16),
            jax.ShapeDtypeStruct((FEAT, WIDTH), BF16),
            jax.ShapeDtypeStruct((FEAT, WIDTH), BF16),
            jax.ShapeDtypeStruct((WIDTH, FEAT), BF16),
        ],
        in_specs=[pl.BlockSpec(memory_space=pltpu.SMEM), vmem, vmem, hbm, hbm, hbm],
        out_specs=[vmem, hbm, hbm, hbm],
        scratch_shapes=[
            pltpu.VMEM((FEAT, WIDTH), BF16),
            pltpu.VMEM((FEAT, WIDTH), BF16),
            pltpu.VMEM((WIDTH, FEAT), BF16),
            pltpu.VMEM((64, FEAT), BF16),
            pltpu.VMEM((64, FEAT), BF16),
            pltpu.VMEM((2, UNITS, CHIPS, 16, FEAT), BF16),
            pltpu.VMEM((UNITS, 3, TOK, WIDTH), F32),
            pltpu.VMEM((UNITS, 3, TOK, WIDTH), BF16),
            pltpu.VMEM((UNITS, 2, 3, 16, WIDTH), BF16),
            pltpu.VMEM((UNITS, 2, 3, 32, WIDTH), BF16),
            pltpu.VMEM((UNITS, 2, 3, 16, WIDTH // 2), F32),
            pltpu.VMEM((UNITS, 3, 16, WIDTH), BF16),
            pltpu.VMEM((UNITS, 3, 16, WIDTH), BF16),
            pltpu.VMEM((UNITS, 3, TOK, WIDTH), BF16),
            pltpu.VMEM((UNITS, 2, TOK, TILE), F32),
            pltpu.VMEM((UNITS, TOK, TILE), F32),
            pltpu.VMEM((UNITS, CHIPS, 16, TILE), F32),
            pltpu.VMEM((UNITS, 16, TILE), F32),
            pltpu.VMEM((UNITS, 8, TILE), F32),
            pltpu.VMEM((FEAT, UNITS * TOK), BF16),
            pltpu.VMEM((FEAT, WIDTH), BF16),
            pltpu.VMEM((FEAT, WIDTH), BF16),
            pltpu.VMEM((WIDTH, FEAT), BF16),
            dma((3,)),
            dma((3, WIDTH // TILE)),
            dma((2, 10)),
            dma((2, 10)),
            dma((UNITS, len(SPANS), 19)),
            dma((UNITS, len(SPANS), 19)),
            dma((UNITS, 8)),
            dma((UNITS, 9)),
        ],
        compiler_params=pltpu.CompilerParams(
            collective_id=0, has_side_effects=True, vmem_limit_bytes=56 * 1024 * 1024
        ),
    )(levels, activations, out_grad, w_gate, w_up, w_down)


def settle_kernel(*refs):
    sources, results, stages, sem = refs[:4], refs[4:8], refs[8:12], refs[12]
    loads, stores = [], []
    for src, stage, dst in zip(sources, stages, results):
        pieces = 1 if src.shape[0] == UNITS else COPIES
        size = src.shape[0] // pieces
        for i in range(pieces):
            rows = pl.ds(i * size, size)
            loads.append(pltpu.make_async_copy(src.at[rows], stage.at[rows], sem.at[0, len(loads)]))
            stores.append(pltpu.make_async_copy(stage.at[rows], dst.at[rows], sem.at[1, len(stores)]))
    for load in loads:
        load.start()
    for load, store in zip(loads, stores):
        load.wait()
        store.start()
    for store in stores:
        store.wait()


def settle(*arrays):
    hbm = pl.BlockSpec(memory_space=pl.ANY)
    return pl.pallas_call(
        settle_kernel,
        out_shape=[jax.ShapeDtypeStruct(array.shape, array.dtype) for array in arrays],
        in_specs=[hbm] * 4,
        out_specs=[hbm] * 4,
        scratch_shapes=[pltpu.VMEM(array.shape, array.dtype) for array in arrays]
        + [pltpu.SemaphoreType.DMA((2, 1 + 3 * COPIES))],
        compiler_params=pltpu.CompilerParams(vmem_limit_bytes=60 * 1024 * 1024),
        cost_estimate=pl.CostEstimate(flops=0, bytes_accessed=2 * 5570560, transcendentals=0),
    )(*arrays)


def body(activations, out_grad, w_gate, w_up, w_down, levels):
    return settle(*exchange(levels, activations, out_grad, w_gate, w_up, w_down))


def solution(mesh):
    placed = (
        P(None, "hidden", "dp"),
        P(None, "hidden", "dp"),
        P("dp", "hidden"),
        P("dp", "hidden"),
        P("hidden", "dp"),
        P(),
    )
    return jax.shard_map(
        body,
        mesh=mesh,
        in_specs=placed,
        out_specs=(
            P(None, "hidden", "dp"),
            P("dp", "hidden"),
            P("dp", "hidden"),
            P("hidden", "dp"),
        ),
        check_vma=False,
    )
```

```python
import jax
import jax.numpy as jnp
from jax import lax
from jax.experimental import pallas as pl
from jax.experimental.pallas import tpu as pltpu
from jax.sharding import PartitionSpec as P

MESH = pl.DeviceIdType.MESH
BF16 = jnp.bfloat16
F32 = jnp.float32

UNITS = 4
TOK = 128
FEAT = 512
WIDTH = 1792
TILE = 256
CHIPS = 8
SPANS = ((0, 256), (256, 256), (512, 256), (768, 256), (1024, 256), (1280, 256), (1536, 256))
LENT = {(3, 0): 1, (3, 1): 3, (3, 2): 2, (3, 3): 1, (3, 4): 3, (3, 5): 2, (3, 6): 3, (2, 0): 1, (2, 1): 3}
NT = (((1,), (1,)), ((), ()))
COLLECT = (1, 4)
COPIES = 4
ORDER_LENDER = (3, 2, 1, 0)
ORDER = (0, 3, 2, 1)
LAGS = (0, 3, 6, 9, 12, 15, 18, 21)


def device(z, y, chip, core):
    return (z * 4 + y, chip * 2 + core)


def active_count(chip):
    return 1 + (chip < 4).astype(jnp.int32) + (chip < 2) + (chip < 1)


def kernel(
    lev, x_ref, g_ref, wg_hbm, wu_hbm, wd_hbm,
    in_grad, gate_hbm, up_hbm, down_hbm,
    wg, wu, wd, own, pair, xg, pf, pb, r1, r2, zr, zs, zx, agb, term, pair_t, hr, fs, fr, xt, gate_v, up_v, down_v,
    w_sem, o_sem, a_send, a_recv, s_send, s_recv, h_send, h_recv,
):
    dp = lax.axis_index("dp")
    hidden = lax.axis_index("hidden")
    z, y = dp // 4, dp % 4
    chip, core = hidden // 2, hidden % 2
    xx, zh = chip // 2, chip % 2
    other = 1 - core
    n = active_count(chip)
    z_pair = z + 1 - 2 * (z % 2)
    inner = jnp.logical_or(z == 1, z == 2)
    outer = jnp.logical_not(inner)
    y_opp, y_right, y_left = (y + 2) % 4, (y + 1) % 4, (y + 3) % 4
    partner = device(z, y, chip, other)
    right, left = device(z, y_right, chip, core), device(z, y_left, chip, core)

    def remote(src, dst, send, recv, target):
        return pltpu.make_async_remote_copy(
            src_ref=src, dst_ref=dst, send_sem=send, recv_sem=recv, device_id=target, device_id_type=MESH
        )

    loads = [
        pltpu.make_async_copy(src, dst, w_sem.at[k])
        for k, (src, dst) in enumerate(((wg_hbm, wg), (wu_hbm, wu), (wd_hbm, wd)))
    ]
    for load in loads:
        load.start()

    barrier = pltpu.get_barrier_semaphore()
    greeted = [partner, right, left]
    greeted += [device((z + k) % 4, y, chip, core) for k in (1, 2, 3)]
    greeted += [device(z, y, (chip + k) % CHIPS, core) for k in range(1, CHIPS)]
    for who in greeted:
        pl.semaphore_signal(barrier, inc=1, device_id=who, device_id_type=MESH)

    for array, ref in enumerate((x_ref, g_ref)):
        rows = []
        for u in range(UNITS):
            index = jnp.int32(0)
            for i in range(1, UNITS):
                index = jnp.where(lev[i] == UNITS - 1 - u, i, index)
            rows.append(ref[index].astype(F32))
        own[array * 32 : array * 32 + 16] = jnp.concatenate(rows[:2], 0).astype(BF16)
        own[array * 32 + 16 : array * 32 + 32] = jnp.concatenate(rows[2:], 0).astype(BF16)

    for u in range(UNITS):
        term[u] = jnp.zeros((2, TOK, TILE), F32)

    pl.semaphore_wait(barrier, len(greeted))

    far = 2 * xx + (1 - zh)

    def pair_copy(part):
        rows = pl.ds(pl.multiple_of(other * 32 + part * 16, 16), 16)
        return remote(own.at[rows], pair.at[rows], a_send.at[part, 0], a_recv.at[part, 0], partner)

    def block(part, c):
        return xg.at[core, pl.ds(part * 2, 2), c]

    def gather_z(part):
        ref = block(part, chip)
        return remote(ref, ref, a_send.at[part, 1], a_recv.at[part, 1], device(z, y, far, core))

    def gather_x(part, c, k, slot):
        ref = block(part, c)
        target = device(z, y, 2 * ((xx + k) % 4) + zh, core)
        return remote(ref, ref, a_send.at[part, slot], a_recv.at[part, slot], target)

    def swap(part):
        ref = xg.at[core, pl.ds(part * 2, 2)]
        return remote(ref, ref, a_send.at[part, 8], a_recv.at[part, 8], partner)

    for part in (1, 0):
        pair_copy(part).start()
    for part in (1, 0):
        pair_copy(part).wait_recv()
        rows = pl.ds(pl.multiple_of(core * 32 + part * 16, 16), 16)
        mine, theirs = own[rows].astype(F32), pair[rows].astype(F32)
        zero = jnp.where(core == 0, mine, theirs)
        one = jnp.where(core == 0, theirs, mine)
        xg[core, 2 * part, chip] = jnp.concatenate([zero[:8], one[:8]], 0).astype(BF16)
        xg[core, 2 * part + 1, chip] = jnp.concatenate([zero[8:], one[8:]], 0).astype(BF16)
        gather_z(part).start()
        for k in (1, 2, 3):
            gather_x(part, chip, k, 1 + k).start()
    for part in (1, 0):
        gather_z(part).wait_recv()
        for k in (1, 2, 3):
            gather_x(part, far, k, 4 + k).start()

    def start_swap(part):
        for k in (1, 2, 3):
            gather_x(part, chip, k, 1 + k).wait_recv()
            gather_x(part, far, k, 4 + k).wait_recv()
        swap(part).start()

    start_swap(1)

    @pl.when(xx != 0)
    def _():
        start_swap(0)
        swap(0).wait_recv()

    swap(1).wait_recv()
    for load in loads:
        load.wait()

    def piece(zd, q):
        first, width = SPANS[q]
        cols = pl.ds(pl.multiple_of(first + (zd % 2) * (width // 2), 128), width // 2)
        return pl.ds(y * 32 + (zd // 2) * 16, 16), cols

    def copy_of(u, q, kind):
        span = pl.ds(*SPANS[q])
        half_span = pl.ds(SPANS[q][0] // 2, SPANS[q][1] // 2)

        def part(ref, u, yy, half, count=16):
            return ref.at[u, :, pl.ds(yy * 32 + half * 16, count), span]

        if kind == 0:
            src, dst, to = part(pb, u, y_opp, 0), r1.at[u, 0, :, :, span], right
        elif kind == 1:
            src, dst, to = part(pb, u, y_opp, 1), r1.at[u, 1, :, :, span], left
        elif kind == 2:
            src, dst, to = part(pb, u, y_right, 1), r2.at[u, 0, :, pl.ds(16, 16), span], right
        elif kind == 3:
            src, dst, to = part(pb, u, y_left, 0), r2.at[u, 1, :, pl.ds(0, 16), span], left
        elif kind == 4:
            src, dst, to = r1.at[u, 0, :, :, span], r2.at[u, 0, :, pl.ds(0, 16), span], right
        elif kind == 5:
            src, dst, to = r1.at[u, 1, :, :, span], r2.at[u, 1, :, pl.ds(16, 16), span], left
        elif kind == 6:
            rows, cols = piece(z_pair, q)
            src = pf.at[u, :, rows, cols]
            dst, to = zr.at[u, 0, :, :, half_span], device(z_pair, y, chip, core)
        elif kind == 7:
            src, dst, to = zs.at[u, :, :, span], zx.at[u, :, :, span], device(z_pair, y, chip, core)
        elif kind in (8, 9):
            zd = 2 * (1 - z // 2) + kind - 8
            rows, cols = piece(zd, q)
            src = pf.at[u, :, rows, cols]
            dst, to = zr.at[u, 1, :, :, half_span], device(zd, y, chip, core)
        elif kind in (10, 11, 12):
            rows, cols = piece(z, q)
            src = dst = agb.at[u, :, rows, cols]
            to = device((z + kind - 9) % 4, y, chip, core)
        elif kind in (13, 14):
            src = dst = part(agb, u, y, 0, 32)
            to = (right, left)[kind - 13]
        elif kind == 15:
            src = dst = part(agb, u, y_left, 0)
            to = right
        elif kind == 16:
            src = dst = part(agb, u, y_right, 1)
            to = left
        elif kind == 17:
            src = dst = pb.at[u, :, :, span]
            to = device(z, y, 2 * lender(u, q) + zh, core)
        else:
            src = dst = agb.at[u, :, :, span]
            to = device(z, y, zh, core)
        return remote(src, dst, s_send.at[u, q, kind], s_recv.at[u, q, 8 if kind == 9 else kind], to)

    def lender(u, q):
        where = jnp.int32(1)
        for (unit, span), x_to in LENT.items():
            if span == q:
                where = jnp.where(u == unit, x_to, where)
        return where

    def lent(u, q):
        found = jnp.bool_(False)
        for unit, span in LENT:
            if span == q:
                found = jnp.logical_or(found, u == unit)
        return jnp.logical_and(found, jnp.logical_and(xx == 0, u < n))

    def taken(u, q):
        found = jnp.bool_(False)
        for (unit, span), x_to in LENT.items():
            if span == q:
                found = jnp.logical_or(found, jnp.logical_and(u == unit, xx == x_to))
        return jnp.logical_and(found, u < active_count(zh))

    def pair_term(u):
        return remote(term.at[u, other], pair_t.at[u], h_send.at[u, 7], h_recv.at[u, 8], partner)

    def chip_term(u, k):
        target = (chip + k) % CHIPS
        return remote(
            term.at[u, core, pl.ds(target * 16, 16), :], hr.at[u, chip],
            h_send.at[u, k - 1], h_recv.at[u, chip], device(z, y, target, core),
        )

    def dots(u, q):
        def tile(i, _):
            cols = pl.ds(pl.multiple_of(i * TILE, TILE), TILE)
            rows_x = xg[0, u].reshape(TOK, FEAT)
            rows_g = xg[1, u].reshape(TOK, FEAT)
            values = (
                jnp.dot(rows_x, wg[:, cols], preferred_element_type=F32),
                jnp.dot(rows_x, wu[:, cols], preferred_element_type=F32),
                lax.dot_general(rows_g, wd[cols, :], NT, preferred_element_type=F32),
            )
            for k, value in enumerate(values):
                pf[u, k, :, cols] = value
                pb[u, k, :, cols] = value.astype(BF16)
            return 0

        first, width = SPANS[q]
        if q == 0:

            @pl.when(jnp.logical_and(xx == 0, u == UNITS - 2))
            def _():
                start_swap(0)

            @pl.when(jnp.logical_and(xx == 0, u == 1))
            def _():
                swap(0).wait_recv()

        @pl.when(u < n)
        def _():
            lax.fori_loop(first // TILE, (first + width) // TILE, tile, 0)

        @pl.when(lent(u, q))
        def _():
            copy_of(u, q, 17).start()

        @pl.when(taken(u, q))
        def _():
            copy_of(u, q, 17).wait_recv()
            for k in range(3):
                pf[u, k, :, first : first + width] = pb[u, k, :, first : first + width].astype(F32)

        @pl.when(jnp.logical_not(lent(u, q)))
        def _():
            for kind in range(4):
                copy_of(u, q, kind).start()

    def accumulate(u, q):
        span = pl.ds(*SPANS[q])
        for side, (kind, yy) in enumerate(((0, y_right), (1, y_left))):
            copy_of(u, q, kind).wait_recv()
            rows = pl.ds(yy * 32 + side * 16, 16)
            for k in range(3):
                r1[u, side, k, :, span] = (r1[u, side, k, :, span].astype(F32) + pf[u, k, rows, span]).astype(BF16)
            copy_of(u, q, kind + 4).start()

    def sum_y(u, q):
        span = pl.ds(*SPANS[q])
        for kind in (2, 3, 4, 5):
            copy_of(u, q, kind).wait_recv()
        rows = pl.ds(y * 32, 32)
        for k in range(3):
            pf[u, k, rows, span] += r2[u, 0, k, :, span].astype(F32) + r2[u, 1, k, :, span].astype(F32)
        copy_of(u, q, 6).start()

        @pl.when(outer)
        def _():
            across = pl.ds(y * 32 + (1 - z // 2) * 16, 16)
            for k in range(3):
                zs[u, k, :, span] = pf[u, k, across, span].astype(BF16)
            copy_of(u, q, 7).start()

    def sum_pair(u, q):
        @pl.when(inner)
        def _():
            span = pl.ds(*SPANS[q])
            across = pl.ds(y * 32 + (1 - z // 2) * 16, 16)
            copy_of(u, q, 7).wait_recv()
            for k in range(3):
                pf[u, k, across, span] += zx[u, k, :, span].astype(F32)
            for kind in (8, 9):
                copy_of(u, q, kind).start()

    def units(u, q):
        for kind in (6, 8):
            copy_of(u, q, kind).wait_recv()
        rows, cols = piece(z, q)
        half_span = pl.ds(SPANS[q][0] // 2, SPANS[q][1] // 2)
        gate, up, grad = (
            pf[u, k, rows, cols] + (zr[u, 0, k, :, half_span] + zr[u, 1, k, :, half_span]) for k in range(3)
        )
        s = jax.nn.sigmoid(gate)
        agb[u, 0, rows, cols] = (gate * s * up).astype(BF16)
        agb[u, 1, rows, cols] = (grad * up * s * (1.0 + gate * (1.0 - s))).astype(BF16)
        agb[u, 2, rows, cols] = (grad * gate * s).astype(BF16)
        for kind in (10, 11, 12):
            copy_of(u, q, kind).start()

    def spread_y(u, q):
        for kind in (10, 11, 12):
            copy_of(u, q, kind).wait_recv()
        for kind in (13, 14):
            copy_of(u, q, kind).start()

    def forward_y(u, q):
        for kind in (13, 14):
            copy_of(u, q, kind).wait_recv()
            copy_of(u, q, kind + 2).start()

    def add_term(u, q):
        first, width = SPANS[q]
        span = slice(first, first + width)
        for half in range(2):
            feats = slice(half * TILE, half * TILE + TILE)
            term[u, half] += lax.dot_general(
                agb[u, 1, :, span], wg[feats, span], NT, preferred_element_type=F32
            ) + lax.dot_general(agb[u, 2, :, span], wu[feats, span], NT, preferred_element_type=F32)

    def back(u, q):
        for kind in (15, 16):
            copy_of(u, q, kind).wait_recv()

        @pl.when(taken(u, q))
        def _():
            copy_of(u, q, 18).start()

        @pl.when(jnp.logical_not(taken(u, q)))
        def _():
            add_term(u, q)

    def finish(u):
        pair_term(u).start()

    def send_terms(u):
        pair_term(u).wait_recv()
        term[u, core] += pair_t[u]
        for k in range(1, CHIPS):
            chip_term(u, k).start()

    stages = (dots, accumulate, sum_y, sum_pair, units, spread_y, forward_y, back)
    spans = len(SPANS)

    def unit_at(turn):
        u = jnp.int32(0)
        for index, (first, second) in enumerate(zip(ORDER, ORDER_LENDER)):
            u = jnp.where(turn == index, jnp.where(xx == 0, second, first), u)
        return u

    turns = UNITS + (LAGS[-1] + spans - 1) // spans
    lent_units = sorted({unit for unit, _ in LENT}, reverse=True)

    def collect(unit):
        for q in range(spans):
            if (unit, q) in LENT:

                @pl.when(lent(unit, q))
                def _(unit=unit, q=q):
                    copy_of(unit, q, 18).wait_recv()
                    add_term(unit, q)

        @pl.when(any_lent(unit))
        def _():
            finish(unit)

    def step(t, _):
        @pl.when(t == turns - 2)
        def _():
            xt[...] = xg[0].reshape(UNITS * TOK, FEAT).T

        for q_now in range(spans):
            for unit, place in zip(lent_units, COLLECT):
                if q_now == place:

                    @pl.when(t == turns - 1)
                    def _(unit=unit):
                        collect(unit)

            for lag in reversed(range(len(stages))):
                q = (q_now - LAGS[lag]) % spans
                turn = t + (q_now - LAGS[lag]) // spans
                u = unit_at(turn)
                here = jnp.logical_and(turn >= 0, turn < UNITS)
                mine = jnp.logical_or(u < n, taken(u, q))
                if lag > 0:
                    mine = jnp.logical_and(mine, jnp.logical_not(lent(u, q)))

                @pl.when(jnp.logical_and(here, mine))
                def _(u=u, q=q, lag=lag):
                    stages[lag](u, q)

                if lag == len(stages) - 1 and q == spans - 1:

                    @pl.when(jnp.logical_and(here, jnp.logical_and(u < n, jnp.logical_not(any_lent(u)))))
                    def _(u=u):
                        finish(u)

        return 0

    def any_lent(u):
        found = lent(u, 0)
        for q in range(1, spans):
            found = jnp.logical_or(found, lent(u, q))
        return found

    lax.fori_loop(0, turns, step, 0)

    def spread_terms(i, _):
        send_terms(n - 1 - i)
        return 0

    lax.fori_loop(0, n, spread_terms, 0)

    def clear(u, _):
        for q in range(spans):

            @pl.when(taken(u, q))
            def _(q=q):
                copy_of(u, q, 18).wait_send()
                for kind in range(10, 17):
                    copy_of(u, q, kind).wait_send()

        agb[u] = jnp.zeros((3, TOK, WIDTH), BF16)
        return 0

    lax.fori_loop(n, UNITS, clear, 0)

    def store(i, k):
        cols = pl.ds(pl.multiple_of(i * TILE, TILE), TILE)
        if k == 2:
            return pltpu.make_async_copy(down_v.at[cols, :], down_hbm.at[cols, :], o_sem.at[k, i])
        src, dst = ((gate_v, gate_hbm), (up_v, up_hbm))[k]
        return pltpu.make_async_copy(src.at[:, cols], dst.at[:, cols], o_sem.at[k, i])

    def weights(i, _):
        cols = pl.ds(pl.multiple_of(i * TILE, TILE), TILE)
        act, dgate, dup = (agb[:, k, :, cols].reshape(UNITS * TOK, TILE) for k in range(3))
        gate_v[:, cols] = jnp.dot(xt[...], dgate, preferred_element_type=F32).astype(BF16)
        store(i, 0).start()
        up_v[:, cols] = jnp.dot(xt[...], dup, preferred_element_type=F32).astype(BF16)
        store(i, 1).start()
        down_v[cols, :] = lax.dot_general(
            act, xg[1].reshape(UNITS * TOK, FEAT), (((0,), (0,)), ((), ())), preferred_element_type=F32
        ).astype(BF16)
        store(i, 2).start()
        return 0

    lax.fori_loop(0, WIDTH // TILE, weights, 0)

    for u in range(UNITS):
        fs[u] = jnp.zeros((16, TILE), F32)

        def add(j, _, u=u):
            @pl.when(j == chip)
            def _():
                fs[u] += term[u, core, pl.ds(chip * 16, 16), :]

            @pl.when(j != chip)
            def _():
                remote(
                    hr.at[u, j], hr.at[u, j], h_send.at[u, 0], h_recv.at[u, j], device(z, y, j, core)
                ).wait_recv()
                fs[u] += hr[u, j]

            return 0

        lax.fori_loop(0, (8, 4, 2, 1)[u], add, 0)

    last = remote(
        fs.at[:, pl.ds(pl.multiple_of(other * 8, 8), 8), :], fr, a_send.at[0, 9], a_recv.at[0, 9], partner
    )
    last.start()
    last.wait()
    here = pl.ds(pl.multiple_of(core * TILE, TILE), TILE)
    there = pl.ds(pl.multiple_of(other * TILE, TILE), TILE)
    mine = pl.ds(pl.multiple_of(core * 8, 8), 8)
    for b in range(UNITS):
        u = UNITS - 1 - lev[b]
        in_grad[b, :, here] = fs[u, mine, :].astype(BF16)
        in_grad[b, :, there] = fr[u].astype(BF16)

    def drain(u, _):
        pair_term(u).wait_send()
        for k in range(1, CHIPS):
            chip_term(u, k).wait_send()
        return 0

    lax.fori_loop(0, n, drain, 0)
    for part in (1, 0):
        pair_copy(part).wait_send()
        gather_z(part).wait_send()
        for k in (1, 2, 3):
            gather_x(part, chip, k, 1 + k).wait_send()
            gather_x(part, far, k, 4 + k).wait_send()
        swap(part).wait_send()

    def drain_sums(u, _):
        for q in range(spans):

            @pl.when(lent(u, q))
            def _(q=q):
                copy_of(u, q, 17).wait_send()

            @pl.when(jnp.logical_or(taken(u, q), jnp.logical_and(u < n, jnp.logical_not(lent(u, q)))))
            def _(q=q):
                for kind in range(7):
                    copy_of(u, q, kind).wait_send()

                @pl.when(outer)
                def _():
                    copy_of(u, q, 7).wait_send()

                @pl.when(inner)
                def _():
                    for kind in (8, 9):
                        copy_of(u, q, kind).wait_send()

            @pl.when(jnp.logical_and(u < n, jnp.logical_not(lent(u, q))))
            def _(q=q):
                for kind in range(10, 17):
                    copy_of(u, q, kind).wait_send()

        return 0

    lax.fori_loop(0, UNITS, drain_sums, 0)
    for i in range(WIDTH // TILE):
        for k in range(3):
            store(i, k).wait()


def exchange(levels, activations, out_grad, w_gate, w_up, w_down):
    vmem = pl.BlockSpec(memory_space=pltpu.VMEM)
    hbm = pl.BlockSpec(memory_space=pl.ANY)
    dma = pltpu.SemaphoreType.DMA
    return pl.pallas_call(
        kernel,
        out_shape=[
            jax.ShapeDtypeStruct(activations.shape, BF16),
            jax.ShapeDtypeStruct((FEAT, WIDTH), BF16),
            jax.ShapeDtypeStruct((FEAT, WIDTH), BF16),
            jax.ShapeDtypeStruct((WIDTH, FEAT), BF16),
        ],
        in_specs=[pl.BlockSpec(memory_space=pltpu.SMEM), vmem, vmem, hbm, hbm, hbm],
        out_specs=[vmem, hbm, hbm, hbm],
        scratch_shapes=[
            pltpu.VMEM((FEAT, WIDTH), BF16),
            pltpu.VMEM((FEAT, WIDTH), BF16),
            pltpu.VMEM((WIDTH, FEAT), BF16),
            pltpu.VMEM((64, FEAT), BF16),
            pltpu.VMEM((64, FEAT), BF16),
            pltpu.VMEM((2, UNITS, CHIPS, 16, FEAT), BF16),
            pltpu.VMEM((UNITS, 3, TOK, WIDTH), F32),
            pltpu.VMEM((UNITS, 3, TOK, WIDTH), BF16),
            pltpu.VMEM((UNITS, 2, 3, 16, WIDTH), BF16),
            pltpu.VMEM((UNITS, 2, 3, 32, WIDTH), BF16),
            pltpu.VMEM((UNITS, 2, 3, 16, WIDTH // 2), F32),
            pltpu.VMEM((UNITS, 3, 16, WIDTH), BF16),
            pltpu.VMEM((UNITS, 3, 16, WIDTH), BF16),
            pltpu.VMEM((UNITS, 3, TOK, WIDTH), BF16),
            pltpu.VMEM((UNITS, 2, TOK, TILE), F32),
            pltpu.VMEM((UNITS, TOK, TILE), F32),
            pltpu.VMEM((UNITS, CHIPS, 16, TILE), F32),
            pltpu.VMEM((UNITS, 16, TILE), F32),
            pltpu.VMEM((UNITS, 8, TILE), F32),
            pltpu.VMEM((FEAT, UNITS * TOK), BF16),
            pltpu.VMEM((FEAT, WIDTH), BF16),
            pltpu.VMEM((FEAT, WIDTH), BF16),
            pltpu.VMEM((WIDTH, FEAT), BF16),
            dma((3,)),
            dma((3, WIDTH // TILE)),
            dma((2, 10)),
            dma((2, 10)),
            dma((UNITS, len(SPANS), 19)),
            dma((UNITS, len(SPANS), 19)),
            dma((UNITS, 8)),
            dma((UNITS, 9)),
        ],
        compiler_params=pltpu.CompilerParams(
            collective_id=0, has_side_effects=True, vmem_limit_bytes=56 * 1024 * 1024
        ),
    )(levels, activations, out_grad, w_gate, w_up, w_down)


def settle_kernel(*refs):
    sources, results, stages, sem = refs[:4], refs[4:8], refs[8:12], refs[12]
    loads, stores = [], []
    for src, stage, dst in zip(sources, stages, results):
        pieces = 1 if src.shape[0] == UNITS else COPIES
        size = src.shape[0] // pieces
        for i in range(pieces):
            rows = pl.ds(i * size, size)
            loads.append(pltpu.make_async_copy(src.at[rows], stage.at[rows], sem.at[0, len(loads)]))
            stores.append(pltpu.make_async_copy(stage.at[rows], dst.at[rows], sem.at[1, len(stores)]))
    for load in loads:
        load.start()
    for load, store in zip(loads, stores):
        load.wait()
        store.start()
    for store in stores:
        store.wait()


def settle(*arrays):
    hbm = pl.BlockSpec(memory_space=pl.ANY)
    return pl.pallas_call(
        settle_kernel,
        out_shape=[jax.ShapeDtypeStruct(array.shape, array.dtype) for array in arrays],
        in_specs=[hbm] * 4,
        out_specs=[hbm] * 4,
        scratch_shapes=[pltpu.VMEM(array.shape, array.dtype) for array in arrays]
        + [pltpu.SemaphoreType.DMA((2, 1 + 3 * COPIES))],
        compiler_params=pltpu.CompilerParams(vmem_limit_bytes=60 * 1024 * 1024),
        cost_estimate=pl.CostEstimate(flops=0, bytes_accessed=2 * 5570560, transcendentals=0),
    )(*arrays)


def body(activations, out_grad, w_gate, w_up, w_down, levels):
    return settle(*exchange(levels, activations, out_grad, w_gate, w_up, w_down))


def solution(mesh):
    placed = (
        P(None, "hidden", "dp"),
        P(None, "hidden", "dp"),
        P("dp", "hidden"),
        P("dp", "hidden"),
        P("hidden", "dp"),
        P(),
    )
    return jax.shard_map(
        body,
        mesh=mesh,
        in_specs=placed,
        out_specs=(
            P(None, "hidden", "dp"),
            P("dp", "hidden"),
            P("dp", "hidden"),
            P("hidden", "dp"),
        ),
        check_vma=False,
    )
```
